1024 devices in a mesh: blk: 16 (over z), rep: 16 (over x_lo, y), pair: 4 (over x_hi, core).
Axes of the slice: x: 4 (x_hi: 2, x_lo: 2; x = x_hi * 2 + x_lo), y: 8, z: 16, core: 2. Of those that a mesh axis runs over, the one named last changes fastest.
Arguments:
- tokens: bfloat16 [163840, 4096], P(('blk', 'rep', 'pair')), may hold values from -24 to 24
- cotangent: bfloat16 [163840, 4096], P(('blk', 'rep', 'pair')), may hold values from -0.0390625 to 0.0390625
- gate_weight: bfloat16 [4096, 3584], P(None, 'blk'), may hold values from -0.09375 to 0.09375
- up_weight: bfloat16 [4096, 3584], P(None, 'blk'), may hold values from -0.09375 to 0.09375
- down_weight: bfloat16 [3584, 4096], P('blk'), may hold values from -0.25 to 0.25
- lengths: int32 [1024, 4], P(('blk', 'rep', 'pair')), may hold values from 1 to 157, as said below
- rewards: int32 [1024, 4], P(('blk', 'rep', 'pair')), may hold values from -65536 to 65536
Outputs:
- grad_gate: float32 [4096, 3584], P(('rep', 'pair'), 'blk')
- grad_up: float32 [4096, 3584], P(('rep', 'pair'), 'blk')
The draws below stay inside these ranges and needn't reach their ends.
Inputs may be any that keep to these rules, and one draw needn't show every extreme that they name: `lengths`: every completion has at least one token. A device's live tokens fill its first rows; their count is at most 160 and equals 160 on some device. Two devices whose pair indices differ only in the lowest bit hold together at most 256 live tokens, and exactly that many for some such two.
All inputs are finite; a program needn't handle non-finite values.
Results may differ from the reference program's by a relative error of at most 0.024.
Values may be sent and summed in bfloat16 or wider, within the bound.
No kernel may reach another device: no remote copies, remote signals or barrier semaphores. Data moves between devices by JAX's collectives and lax.ppermute only.
A program may use at most 64 MiB of HBM per device.

```python
import jax
import jax.numpy as jnp
from jax import lax

D = 4096
HB = 224
COMP = 4
CAP = 128
SLOTS = 160
HOLDERS = 1024
TOKENS = 163840
HID = 3584
N_BLK = 16
N_REP = 16
N_PAIR = 4


def draw_lengths(key, part):
    key = jax.random.fold_in(key, 7)
    subkeys = jax.random.split(key, 5)
    couples = HOLDERS // 2
    lowest = 2 * CAP - SLOTS
    heavier = CAP + jax.random.randint(subkeys[0], (couples,), 0, SLOTS - CAP + 1)
    spread = 2 * CAP - heavier - lowest + 1
    lighter = lowest + jax.random.randint(subkeys[1], (couples,), 0, 1 << 20) % spread
    chosen = jax.random.randint(subkeys[2], (), 0, couples)
    marked = jnp.arange(couples) == chosen
    heavier = jnp.where(marked, SLOTS, heavier)
    lighter = jnp.where(marked, lowest, lighter)
    flipped = jax.random.randint(subkeys[3], (couples,), 0, 2) == 1
    former = jnp.where(flipped, heavier, lighter)
    latter = jnp.where(flipped, lighter, heavier)
    totals = jnp.stack([former, latter], axis=1).reshape(HOLDERS)
    full_device = jnp.repeat(marked, 2) & (totals == SLOTS)
    cut_points = jax.random.randint(subkeys[4], (HOLDERS, COMP - 1), 0, 1 << 20) % (totals - COMP + 1)[:, None]
    cut_points = jnp.where(full_device[:, None], 0, cut_points)
    cut_points = jnp.sort(cut_points, axis=1)
    boundaries = jnp.concatenate([jnp.zeros((HOLDERS, 1), jnp.int32), cut_points, (totals - COMP)[:, None]], axis=1)
    return (jnp.diff(boundaries, axis=1) + 1).astype(jnp.int32)


def plant(result, rng, smallest, top_value):
    longest = result.shape.index(max(result.shape))
    spots = []
    for shift in (0, 1):
        where = [jax.random.randint(jax.random.fold_in(rng, axis), (), 0, length) for axis, length in enumerate(result.shape)]
        where[longest] = (where[longest] + shift) % result.shape[longest]
        spots.append(tuple(where))
    return result.at[spots[0]].set(smallest).at[spots[1]].set(top_value)


def raised(result, key, source, target, shards_of, factor):
    def block_of(dim):
        return (jnp.arange(result.shape[dim]) // (result.shape[dim] // shards_of)).reshape((-1,) + (1,) * (result.ndim - 1 - dim))

    first = jax.random.permutation(key, shards_of)[block_of(target)]
    second = (block_of(target) + shards_of // 2) % shards_of
    return jnp.where((block_of(source) == first) | (block_of(source) == second), factor * result, result)


def block_levels(key, extent, cuts, least, largest):
    level, own = 1.0, jax.random.fold_in(key, 6)
    for dim, blocks in cuts:
        steps = jnp.exp(jax.random.uniform(jax.random.fold_in(own, dim), (blocks,), jnp.float32, least / len(cuts), largest / len(cuts)))
        level = level * jnp.repeat(steps, extent[dim] // blocks).reshape([-1 if axis == dim else 1 for axis in range(len(extent))])
    return level


def scatter_about(own_key, shape, deviation, most, cuts=(), kind=jnp.bfloat16):
    result = deviation * jax.random.normal(own_key, shape, jnp.float32)
    if cuts:
        result = result * block_levels(own_key, shape, cuts, -0.22, 0.18)
    return jnp.clip(result, -most, most).astype(kind)


def gaussian_with(own_key, dims, scale, limit, shards, heavy, kind=jnp.bfloat16):
    result = scale * jax.random.normal(own_key, dims, jnp.float32)
    if shards:
        result = result * block_levels(own_key, dims, shards, -0.22, 0.18)
    return jnp.clip(raised(result, jax.random.fold_in(own_key, 3), *heavy), -limit, limit).astype(kind)


def setup_inputs(seed: int = 0) -> dict:
    seeds = jax.random.split(jax.random.key(seed), 8)
    return {
        "tokens": gaussian_with(seeds[0], (TOKENS, D), 1.0, 24.0, ((0, 1024),), (0, 1, 1024, 6.0)),
        "cotangent": scatter_about(seeds[1], (TOKENS, D), (2 * SLOTS * N_REP * N_PAIR) ** -0.5, 0.0390625, ((0, 1024),)),
        "gate_weight": scatter_about(seeds[2], (D, HID), D ** -0.5, 0.09375, ((1, 16),)),
        "up_weight": scatter_about(seeds[3], (D, HID), D ** -0.5, 0.09375, ((1, 16),)),
        "down_weight": scatter_about(seeds[4], (HID, D), (2 * HB) ** -0.5, 0.25, ((0, 16),)),
        "lengths": draw_lengths(jax.random.fold_in(seeds[7], 71), 0),
        "rewards": plant(jax.random.randint(seeds[6], (HOLDERS, COMP), -65536, 65537), jax.random.fold_in(seeds[6], 1), -65536, 65536).astype(jnp.int32),
    }


def row_weights(lengths, rewards, slot_count):
    position = jnp.arange(slot_count, dtype=jnp.int32)
    end_index = jnp.cumsum(lengths, axis=1).astype(jnp.int32)
    starts = end_index - lengths
    inside = (position[None, None, :] >= starts[:, :, None]) & (position[None, None, :] < end_index[:, :, None])
    scaled = rewards.astype(jnp.float32)[:, :, None] / 65536.0
    return jnp.sum(jnp.where(inside, scaled, jnp.zeros_like(scaled)), axis=1)


def pieces(row_block, cot_block, gate_block, up_block, down_block):
    gate_pre = jnp.dot(row_block, gate_block, preferred_element_type=jnp.float32)
    up_pre = jnp.dot(row_block, up_block, preferred_element_type=jnp.float32)
    sigmoid_gate = jax.nn.sigmoid(gate_pre)
    active = gate_pre * sigmoid_gate
    back_hidden = lax.dot_general(cot_block, down_block, (((1,), (1,)), ((), ())), preferred_element_type=jnp.float32)
    gate_back = (back_hidden * up_pre * sigmoid_gate * (1.0 + gate_pre * (1.0 - sigmoid_gate))).astype(jnp.bfloat16)
    up_back = (back_hidden * active).astype(jnp.bfloat16)
    return gate_back, up_back


def contract(left_side, right_side):
    return lax.dot_general(left_side, right_side, (((0,), (0,)), ((), ())), preferred_element_type=jnp.float32)


def reference(tokens, cotangent, gate_weight, up_weight, down_weight, lengths, rewards):
    members = N_REP * N_PAIR
    weight = row_weights(lengths, rewards, SLOTS).reshape(N_BLK, members, SLOTS)
    token_groups = tokens.reshape(N_BLK, members, SLOTS, D)
    cot_groups = cotangent.reshape(N_BLK, members, SLOTS, D)
    gate_blocks = gate_weight.reshape(D, N_BLK, HB).transpose(1, 0, 2)
    up_blocks = up_weight.reshape(D, N_BLK, HB).transpose(1, 0, 2)
    down_blocks = down_weight.reshape(N_BLK, HB, D)

    def weigh(block_index, member):
        row_scale = weight[block_index, member]
        return (row_scale[:, None] * cot_groups[block_index, member].astype(jnp.float32)).astype(jnp.bfloat16)

    def one_block(block_index):
        behind = (block_index + N_BLK - 1) % N_BLK
        gate_block = gate_blocks[block_index]
        up_block = up_blocks[block_index]
        down_block = down_blocks[block_index]

        def add_member(totals, member):
            all_rows = jnp.concatenate([token_groups[block_index, member], token_groups[behind, member]], axis=0)
            all_cot = jnp.concatenate([weigh(block_index, member), weigh(behind, member)], axis=0)
            gate_back, up_back = pieces(all_rows, all_cot, gate_block, up_block, down_block)
            partial_terms = (contract(all_rows, gate_back), contract(all_rows, up_back))
            rounded = tuple(lax.optimization_barrier(term.astype(jnp.bfloat16)).astype(jnp.float32) for term in partial_terms)
            return tuple(total + extra for total, extra in zip(totals, rounded)), None

        initial = (jnp.zeros((D, HB), jnp.float32), jnp.zeros((D, HB), jnp.float32))
        totals, _ = lax.scan(add_member, initial, jnp.arange(members, dtype=jnp.int32))
        return totals

    gate_grads, up_grads = lax.map(one_block, jnp.arange(N_BLK, dtype=jnp.int32))
    grad_gate = gate_grads.transpose(1, 0, 2).reshape(D, N_BLK * HB)
    grad_up = up_grads.transpose(1, 0, 2).reshape(D, N_BLK * HB)
    return (grad_gate, grad_up)
```

```python
import jax
import jax.numpy as jnp
from jax import lax
from jax.sharding import Mesh
from jax.sharding import PartitionSpec as P

HB = 224
ROWS = 64


def shifted(block, axis, distance):
    devices = range(lax.axis_size(axis))
    route = [((i - distance) % len(devices), i) for i in devices]
    return lax.ppermute(block, axis, route)


def row_weights(lengths, rewards, slot_count):
    position = jnp.arange(slot_count, dtype=jnp.int32)
    end_index = jnp.cumsum(lengths, axis=1)
    starts = end_index - lengths
    inside = (position[None, None, :] >= starts[:, :, None]) & (
        position[None, None, :] < end_index[:, :, None]
    )
    scaled = rewards.astype(jnp.float32)[:, :, None] / 65536.0
    return jnp.sum(jnp.where(inside, scaled, jnp.zeros_like(scaled)), axis=1)


def pieces(row_block, cot_block, gate_block, up_block, down_block):
    gate_pre = jnp.dot(row_block, gate_block, preferred_element_type=jnp.float32)
    up_pre = jnp.dot(row_block, up_block, preferred_element_type=jnp.float32)
    sigmoid_gate = jax.nn.sigmoid(gate_pre)
    active = gate_pre * sigmoid_gate
    back_hidden = lax.dot_general(
        cot_block, down_block, (((1,), (1,)), ((), ())), preferred_element_type=jnp.float32
    )
    gate_back = (
        back_hidden * up_pre * sigmoid_gate * (1.0 + gate_pre * (1.0 - sigmoid_gate))
    ).astype(jnp.bfloat16)
    up_back = (back_hidden * active).astype(jnp.bfloat16)
    return (gate_back, up_back)


def contract(left_side, right_side):
    return lax.dot_general(
        left_side, right_side, (((0,), (0,)), ((), ())), preferred_element_type=jnp.float32
    )


def on_device(tokens, cotangent, gate_weight, up_weight, down_weight, lengths, rewards):
    row_count = tokens.shape[0]
    weight = row_weights(lengths, rewards, row_count)[0]
    weighted = (weight[:, None] * cotangent.astype(jnp.float32)).astype(jnp.bfloat16)
    far_rows, far_cot = shifted((tokens, weighted), "z", 1)
    all_rows = jnp.concatenate([tokens, far_rows], axis=0)
    all_cot = jnp.concatenate([weighted, far_cot], axis=0)
    gate_back, up_back = pieces(all_rows, all_cot, gate_weight, up_weight, down_weight)
    both = jnp.concatenate([gate_back, up_back], axis=1)
    ordered = all_rows.reshape(-1, 2, 8, 2, 2, ROWS).transpose(0, 4, 2, 3, 1, 5)
    ordered = ordered.reshape(all_rows.shape)
    term = contract(ordered, both).astype(jnp.bfloat16)
    term = lax.psum_scatter(term, "c", scatter_dimension=0, tiled=True)
    term = lax.psum_scatter(term, "y", scatter_dimension=0, tiled=True)
    term = lax.all_to_all(term, ("xh", "xl"), split_axis=0, concat_axis=0, tiled=True)
    total = jnp.sum(term.reshape(4, ROWS, 2 * HB).astype(jnp.float32), axis=0)
    return (total[:, :HB], total[:, HB:])


def solution(mesh):
    fine = Mesh(mesh.devices.reshape(16, 2, 8, 2, 2), ("z", "xl", "y", "xh", "c"))
    rows = P(("z", "xl", "y", "xh", "c"), None)
    placed = (rows, rows, P(None, "z"), P(None, "z"), P("z", None), rows, rows)
    out = P(("xl", "y", "xh", "c"), "z")
    return jax.shard_map(
        on_device, mesh=fine, in_specs=placed, out_specs=(out, out), check_vma=False
    )
```

```python
import functools

import jax
import jax.numpy as jnp
from jax import lax
from jax.experimental import pallas as pl
from jax.experimental.pallas import tpu as pltpu
from jax.sharding import Mesh
from jax.sharding import PartitionSpec as P

D = 4096
HALF = D // 2
HB = 224
SLOTS = 160
CAP = 128
HEAD = 96
TAIL = CAP - HEAD
SPARE = SLOTS - CAP
UP = 256
MARK = 16
FIRST, SECOND = 4, 8
PARTS = 4
BF, F32 = jnp.bfloat16, jnp.float32
VMEM = pl.BlockSpec(memory_space=pltpu.VMEM)
SMEM = pl.BlockSpec(memory_space=pltpu.SMEM)
HBM = pl.BlockSpec(memory_space=pltpu.HBM)


def source_tile(first, second):
    x_hi, x_lo, y = first // 2, first % 2, second
    return (x_lo * 8 + y) * 2 + x_hi


def call(body, outs, scratch=(), room=32, cost=0.0, **more):
    return pl.pallas_call(
        body,
        out_shape=outs,
        scratch_shapes=scratch,
        cost_estimate=pl.CostEstimate(flops=int(cost * 1e10), bytes_accessed=int(cost * 1e6), transcendentals=0),
        compiler_params=pltpu.CompilerParams(vmem_limit_bytes=room * 1024 * 1024),
        **more,
    )


def shape(*dims, kind=BF):
    return jax.ShapeDtypeStruct(dims, kind)


def mm(a, b, dims=((1,), (0,))):
    return lax.dot_general(a, b, (dims, ((), ())), preferred_element_type=F32)


def sorter(core):
    src = lax.broadcasted_iota(jnp.int32, (256, 256), 0)
    dst = lax.broadcasted_iota(jnp.int32, (256, 256), 1)
    lane = dst % 128
    side = jnp.where(dst < 128, core, 1 - core)
    want = (lane // 64) * 128 + side * 64 + lane % 64
    return jnp.where(src == want, 1.0, 0.0).astype(BF)


def column_copies(ref, held, sems):
    copies = []
    for k in range(PARTS):
        at = pl.ds(k * (D // PARTS), D // PARTS)
        copies.append(pltpu.make_async_copy(ref.at[:, at], held.at[:, at], sems.at[k]))
        copies[-1].start()
    return copies


def sorted_tiles(held, perm, copies, scale=None):
    tiles_of = D // 128 // PARTS
    order = sorted(range(HALF // 128), key=lambda k: source_tile(2 * k // SECOND, 2 * k % SECOND + 1))
    here = 0
    for k in order:
        first, second = (2 * k) // SECOND, (2 * k) % SECOND
        one, two = source_tile(first, second), source_tile(first, second + 1)
        while here <= max(one, two) // tiles_of:
            copies[here].wait()
            here += 1
        both = [held[:, t * 128 : (t + 1) * 128] for t in (one, two)]
        if scale is not None:
            both = [(scale * b.astype(F32)).astype(BF) for b in both]
        yield slice(k * 128, (k + 1) * 128), mm(jnp.concatenate(both, axis=1), perm).astype(BF)


def staging(rows):
    return [pltpu.VMEM((rows, D), BF), pltpu.SemaphoreType.DMA((PARTS,))]


def live(len_ref):
    return len_ref[0, 0] + len_ref[0, 1] + len_ref[0, 2] + len_ref[0, 3]


def split_rows(core_ref, len_ref, tok_ref, head_out, rest_out, other_out, held, sems):
    copies = column_copies(tok_ref, held, sems)
    perm = sorter(core_ref[0])
    other_out[SLOTS:, :] = jnp.full((MARK, HALF), live(len_ref), jnp.int32).astype(F32).astype(BF)
    for at, tile in sorted_tiles(held, perm, copies):
        head_out[:, at] = tile[:HEAD, :128]
        rest_out[:, at] = tile[HEAD:, :128]
        other_out[:SLOTS, at] = tile[:, 128:]


def split_down(core_ref, down_ref, down_out, held, sems):
    copies = column_copies(down_ref, held, sems)
    perm = sorter(core_ref[0])
    for at, tile in sorted_tiles(held, perm, copies):
        down_out[:, at] = tile[:, :128]


def split_wide(core_ref, gate_ref, up_ref, wide_out, held, sems, held_up, sems_up):
    copies = column_copies(gate_ref, held, sems)
    copies_up = column_copies(up_ref, held_up, sems_up)
    perm = sorter(core_ref[0])
    wide_out[HB:UP, :] = jnp.zeros((UP - HB, HALF), BF)
    wide_out[UP + HB :, :] = jnp.zeros((UP - HB, HALF), BF)
    for at, tile in sorted_tiles(held, perm, copies):
        wide_out[:HB, at] = tile[:, :128]
    for at, tile in sorted_tiles(held_up, perm, copies_up):
        wide_out[UP : UP + HB, at] = tile[:, :128]


def split_cot(core_ref, len_ref, rew_ref, cot_ref, own_out, other_out, held, sems):
    copies = column_copies(cot_ref, held, sems)
    perm = sorter(core_ref[0])
    row = lax.broadcasted_iota(jnp.int32, (SLOTS, 1), 0)
    weight, start = jnp.zeros((SLOTS, 1), F32), jnp.int32(0)
    for j in range(4):
        end = start + len_ref[0, j]
        scaled = jnp.full((SLOTS, 1), rew_ref[0, j], jnp.int32).astype(F32) / 65536.0
        weight += jnp.where((row >= start) & (row < end), scaled, 0.0)
        start = end
    for at, tile in sorted_tiles(held, perm, copies, weight):
        own_out[:, at] = tile[:, :128]
        other_out[:SLOTS, at] = tile[:, 128:]
    other_out[SLOTS:, :] = jnp.full((MARK, HALF), live(len_ref), jnp.int32).astype(F32).astype(BF)


def merged(tail, surplus, count):
    slot = lax.broadcasted_iota(jnp.int32, (TAIL, TAIL + SPARE), 0)
    src = lax.broadcasted_iota(jnp.int32, (TAIL, TAIL + SPARE), 1)
    want = jnp.where(HEAD + slot < count, slot, TAIL + slot - jnp.maximum(count - HEAD, 0))
    pick = jnp.where(src == want, 1.0, 0.0).astype(BF)
    return mm(pick, jnp.concatenate([tail, surplus], axis=0)).astype(BF)


def other_count(ref):
    mark = ref[SLOTS : SLOTS + MARK, :128].astype(F32)
    return mark[:1, : TAIL + SPARE].astype(jnp.int32)


def merge_rows(len_ref, rest_ref, got_ref, out_ref):
    rest, got = rest_ref[...], got_ref[:SLOTS, :]
    out_ref[:TAIL, :] = merged(rest[:TAIL], got[CAP:], live(len_ref))
    out_ref[TAIL : TAIL + HEAD, :] = got[:HEAD]
    out_ref[TAIL + HEAD :, :] = merged(got[HEAD:CAP], rest[TAIL:], other_count(got_ref))


def near_terms(
    len_ref, head_ref, tail_ref, far_head_ref, own_ref, got_ref, wide_ref, down_ref, cot_out, sum_out
):
    own, got = own_ref[...], got_ref[:SLOTS, :]
    cot_out[:HEAD, :] = own[:HEAD]
    cot_out[HEAD:CAP, :] = merged(own[HEAD:CAP], got[CAP:], live(len_ref))
    cot_out[CAP : CAP + HEAD, :] = got[:HEAD]
    cot_out[CAP + HEAD :, :] = merged(got[HEAD:CAP], own[CAP:], other_count(got_ref))
    rows = jnp.concatenate([head_ref[...], tail_ref[...], far_head_ref[...]], axis=0)
    sum_out[:, : 2 * UP] = mm(rows, wide_ref[...], ((1,), (1,)))
    sum_out[: 2 * CAP, 2 * UP : 2 * UP + HB] = mm(cot_out[...], down_ref[...], ((1,), (1,)))
    sum_out[: 2 * CAP, 2 * UP + HB :] = jnp.zeros((2 * CAP, UP - HB), F32)
    sum_out[2 * CAP :, 2 * UP :] = jnp.zeros((HEAD, UP), F32)


def next_back(cot_ref, down_ref, out_ref):
    out_ref[...] = mm(cot_ref[...], down_ref[...], ((1,), (1,))).astype(out_ref.dtype)


def far_terms(tail_ref, wide_ref, out_ref):
    out_ref[...] = mm(tail_ref[...], wide_ref[...], ((1,), (1,))).astype(out_ref.dtype)


def swapped(value):
    return jnp.concatenate([value[CAP:], value[:CAP]], axis=0)


def hidden_grads(gate, up, back):
    sig = jax.nn.sigmoid(gate)
    gate_back = back * up * sig * (1.0 + gate * (1.0 - sig))
    return gate_back.astype(BF), (back * (gate * sig)).astype(BF)


def near_grads(mine_ref, other_ref, gate_out, up_out, early_out):
    total = mine_ref[: 2 * CAP] + swapped(other_ref[: 2 * CAP])
    gate_out[...], up_out[...] = hidden_grads(
        total[:, :HB], total[:, UP : UP + HB], total[:, 2 * UP : 2 * UP + HB]
    )
    early_out[...] = jnp.zeros_like(early_out)
    early_out[:HEAD] = mine_ref[2 * CAP :, : 2 * UP]
    early_out[CAP : CAP + HEAD] = other_ref[2 * CAP :, : 2 * UP]


def weight_grads(
    early_ref, mine_ref, other_ref, back_ref, cross_ref, gate_ref, up_ref,
    head_ref, tail_ref, far_head_ref, far_tail_ref, out_ref, gate_all, up_all,
):
    @pl.when(pl.program_id(0) == 0)
    def _():
        mine, other = mine_ref[...].astype(F32), other_ref[...].astype(F32)
        early = early_ref[...]
        total = jnp.concatenate(
            [
                early[:HEAD] + other[TAIL : TAIL + HEAD],
                mine[:TAIL] + other[TAIL + HEAD :],
                early[CAP : CAP + HEAD] + mine[TAIL : TAIL + HEAD],
                mine[TAIL + HEAD :] + other[:TAIL],
            ],
            axis=0,
        )
        back = back_ref[...].astype(F32) + swapped(cross_ref[...].astype(F32))
        gate_all[2 * CAP :], up_all[2 * CAP :] = hidden_grads(
            total[:, :HB], total[:, UP : UP + HB], back
        )
        gate_all[: 2 * CAP] = gate_ref[...]
        up_all[: 2 * CAP] = up_ref[...]

    rows = jnp.concatenate(
        [head_ref[...], tail_ref[...], far_head_ref[...], far_tail_ref[...]], axis=0
    )
    out_ref[0, :HB] = mm(gate_all[...], rows, ((0,), (0,))).astype(BF)
    out_ref[0, HB:] = mm(up_all[...], rows, ((0,), (0,))).astype(BF)


def first_sum(in_ref, out_ref):
    total = in_ref[0].astype(F32)
    for k in range(1, FIRST):
        total += in_ref[k].astype(F32)
    lane = lax.broadcasted_iota(jnp.int32, (HB, 128), 1)
    for k in range(SECOND // 2):
        gate = total[:HB, k * 128 : (k + 1) * 128]
        up = total[HB:, k * 128 : (k + 1) * 128]
        out_ref[2 * k] = jnp.where(lane < 64, gate, pltpu.roll(up, 64, 1)).astype(BF)
        out_ref[2 * k + 1] = jnp.where(lane < 64, pltpu.roll(gate, 64, 1), up).astype(BF)


def second_sum(in_ref, gate_out, up_out):
    total = in_ref[0].astype(F32)
    for k in range(1, SECOND):
        total += in_ref[k].astype(F32)
    full = jnp.concatenate([total, jnp.zeros((UP - HB, 128), F32)], axis=0).T
    gate_out[...] = full[:64, :HB]
    up_out[...] = full[64:, :HB]


def along_z(block, distance):
    n = lax.axis_size("z")
    return lax.ppermute(block, "z", [(i, (i + distance) % n) for i in range(n)])


def between_cores(block):
    return lax.ppermute(block, "c", [(0, 1), (1, 0)])


def along_z_crossed(block):
    n = lax.axis_size("z")
    route = [(2 * i + c, 2 * ((i + 1) % n) + 1 - c) for i in range(n) for c in range(2)]
    return lax.ppermute(block, ("z", "c"), route)


def on_device(tokens, cotangent, gate_weight, up_weight, down_weight, lengths, rewards):
    core = lax.axis_index("c").astype(jnp.int32).reshape(1)
    head, rest, row_other = call(
        split_rows,
        (shape(HEAD, HALF), shape(SLOTS - HEAD, HALF), shape(SLOTS + MARK, HALF)),
        in_specs=[SMEM, SMEM, HBM], scratch=staging(SLOTS), cost=1.7,
    )(core, lengths, tokens)
    far_head = along_z(head, 1)
    row_got = between_cores(row_other)
    down = call(
        split_down, shape(HB, HALF), in_specs=[SMEM, HBM], scratch=staging(HB), cost=1.4,
    )(core, down_weight)
    next_down = along_z(down, -1)
    cot_own, cot_other = call(
        split_cot,
        (shape(SLOTS, HALF), shape(SLOTS + MARK, HALF)),
        in_specs=[SMEM, SMEM, SMEM, HBM], scratch=staging(SLOTS), cost=1.8,
    )(core, lengths, rewards, cotangent)
    cot_got = between_cores(cot_other)
    tail = call(
        merge_rows, shape(CAP + TAIL, HALF), cost=0.8,
                in_specs=[SMEM, VMEM, VMEM],
    )(lengths, rest, row_got)
    far_tail = along_z(tail, 1)

    wide = call(
        split_wide, shape(2 * UP, HALF), in_specs=[SMEM, HBM, HBM], scratch=staging(HB) * 2, cost=2.7,
    )(core, gate_weight.T, up_weight.T)
    cot_rows, near = call(
        near_terms,
        (shape(2 * CAP, HALF), shape(2 * CAP + HEAD, 3 * UP, kind=F32)),
        cost=2.3, in_specs=[SMEM] + [VMEM] * 7,
    )(lengths, head, tail, far_head, cot_own, cot_got, wide, down)
    near_other = between_cores(near)
    back = call(
        next_back, shape(2 * CAP, HB), cost=0.5,
                in_specs=[VMEM] * 2,
    )(cot_rows, next_down)
    far_back, far_cross = along_z(back, 1), along_z_crossed(back)
    gate_near, up_near, early = call(
        near_grads,
        (shape(2 * CAP, HB), shape(2 * CAP, HB), shape(2 * CAP, 2 * UP, kind=F32)),
        cost=0.3, in_specs=[VMEM] * 2,
    )(near, near_other)
    far = call(
        far_terms, shape(CAP + TAIL, 2 * UP), cost=0.8, in_specs=[VMEM] * 2
    )(far_tail, wide)
    far_other = between_cores(far)

    cols = HALF // FIRST
    whole = lambda *dims: pl.BlockSpec(dims, lambda i: (0,) * len(dims))
    part = lambda rows: pl.BlockSpec((rows, cols), lambda i: (0, i))
    grads = call(
        weight_grads, shape(FIRST, 2 * HB, cols),
                scratch=[pltpu.VMEM((4 * CAP, HB), BF)] * 2, cost=2.1,
        grid=(FIRST,),
        in_specs=[whole(2 * CAP, 2 * UP)] + [whole(CAP + TAIL, 2 * UP)] * 2 + [whole(2 * CAP, HB)] * 4
        + [part(HEAD), part(CAP + TAIL)] * 2,
        out_specs=pl.BlockSpec((1, 2 * HB, cols), lambda i: (i, 0, 0)),
    )(early, far, far_other, far_back, far_cross, gate_near, up_near, head, tail, far_head, far_tail)
    grads = lax.all_to_all(grads, ("xh", "xl"), split_axis=0, concat_axis=0, tiled=True)
    grads = call(
        first_sum, shape(SECOND, HB, 128), cost=0.4,
    )(grads)
    grads = lax.all_to_all(grads, "y", split_axis=0, concat_axis=0, tiled=True)
    return call(
        second_sum, (shape(64, HB, kind=F32), shape(64, HB, kind=F32)),
                in_specs=[VMEM],
    )(grads)


def solution(mesh):
    planes = mesh.shape["blk"]
    fine = Mesh(mesh.devices.reshape(planes, 2, 8, 2, 2), ("z", "xl", "y", "xh", "c"))
    rows = P(("z", "xl", "y", "xh", "c"), None)
    placed = (rows, rows, P(None, "z"), P(None, "z"), P("z", None), rows, rows)
    out = P(("xl", "y", "xh", "c"), "z")
    return jax.shard_map(
        on_device, mesh=fine, in_specs=placed, out_specs=(out, out), check_vma=False
    )
```

```python
import functools

import jax
import jax.numpy as jnp
from jax import lax
from jax.experimental import pallas as pl
from jax.experimental.pallas import tpu as pltpu
from jax.sharding import Mesh
from jax.sharding import PartitionSpec as P

D = 4096
HALF = D // 2
HB = 224
SLOTS = 160
CAP = 128
HEAD = 96
TAIL = CAP - HEAD
SPARE = SLOTS - CAP
UP = 256
MARK = 16
HH = HB // 2
FIRST, SECOND = 8, 4
ABREAST = 2
BF, F32 = jnp.bfloat16, jnp.float32
VMEM = pl.BlockSpec(memory_space=pltpu.VMEM)
SMEM = pl.BlockSpec(memory_space=pltpu.SMEM)
ANY = pl.BlockSpec(memory_space=pl.ANY)


def source_tile(first, second):
    x_hi, x_lo, y = first // 4, first // 2 % 2, 2 * second + first % 2
    return (x_lo * 8 + y) * 2 + x_hi


def call(body, outs, scratch=(), room=32, cost=0.0, **more):
    return pl.pallas_call(
        body,
        out_shape=outs,
        scratch_shapes=scratch,
        cost_estimate=pl.CostEstimate(flops=int(cost * 1e10), bytes_accessed=int(cost * 1e6), transcendentals=0),
        compiler_params=pltpu.CompilerParams(vmem_limit_bytes=room * 1024 * 1024),
        **more,
    )


def shape(*dims, kind=BF):
    return jax.ShapeDtypeStruct(dims, kind)


def mm(a, b, dims=((1,), (0,))):
    return lax.dot_general(a, b, (dims, ((), ())), preferred_element_type=F32)


def sorter(core):
    src = lax.broadcasted_iota(jnp.int32, (256, 256), 0)
    dst = lax.broadcasted_iota(jnp.int32, (256, 256), 1)
    lane = dst % 128
    side = jnp.where(dst < 128, core, 1 - core)
    want = (lane // 64) * 128 + side * 64 + lane % 64
    return jnp.where(src == want, 1.0, 0.0).astype(BF)


def sorted_tiles(ref, perm):
    for k in range(HALF // 128):
        first, second = (2 * k) // SECOND, (2 * k) % SECOND
        both = [
            ref[:, t * 128 : (t + 1) * 128]
            for t in (source_tile(first, second), source_tile(first, second + 1))
        ]
        yield slice(k * 128, (k + 1) * 128), mm(jnp.concatenate(both, axis=1), perm).astype(BF)


def mark(len_ref, columns):
    return jnp.full((MARK, columns), live(len_ref), jnp.int32).astype(F32).astype(BF)


def live(len_ref):
    return len_ref[0, 0] + len_ref[0, 1] + len_ref[0, 2] + len_ref[0, 3]


def split_rows(core_ref, len_ref, tok_ref, head_out, rest_out, other_out):
    perm = sorter(core_ref[0])
    other_out[SLOTS:, :] = mark(len_ref, HALF)
    for at, tile in sorted_tiles(tok_ref, perm):
        head_out[:, at] = tile[:HEAD, :128]
        rest_out[:, at] = tile[HEAD:, :128]
        other_out[:SLOTS, at] = tile[:, 128:]


def split_wide(core_ref, gate_ref, up_ref, after_ref, wide_out):
    perm = sorter(core_ref[0])
    wide_out[HB:UP, :] = jnp.zeros((UP - HB, HALF), BF)
    wide_out[UP + HB :, :] = jnp.zeros((UP - HB, HALF), BF)
    for at, tile in sorted_tiles(gate_ref, perm):
        wide_out[:HB, at] = tile[:, :128]
    for at, tile in sorted_tiles(up_ref, perm):
        wide_out[UP : UP + HB, at] = tile[:, :128]


def weigh(len_ref, rew_ref, cot_ref, after_ref, out_ref):
    row = lax.broadcasted_iota(jnp.int32, (SLOTS, 1), 0)
    weight, start = jnp.zeros((SLOTS, 1), F32), jnp.int32(0)
    for j in range(4):
        end = start + len_ref[0, j]
        scaled = jnp.full((SLOTS, 1), rew_ref[0, j], jnp.int32).astype(F32) / 65536.0
        weight += jnp.where((row >= start) & (row < end), scaled, 0.0)
        start = end
    out_ref[:SLOTS, :] = (weight * cot_ref[...].astype(F32)).astype(BF)
    out_ref[SLOTS:, :] = mark(len_ref, D)


def merged(tail, surplus, count):
    slot = lax.broadcasted_iota(jnp.int32, (TAIL, TAIL + SPARE), 0)
    src = lax.broadcasted_iota(jnp.int32, (TAIL, TAIL + SPARE), 1)
    want = jnp.where(HEAD + slot < count, slot, TAIL + slot - jnp.maximum(count - HEAD, 0))
    pick = jnp.where(src == want, 1.0, 0.0).astype(BF)
    return mm(pick, jnp.concatenate([tail, surplus], axis=0)).astype(BF)


def other_count(ref):
    rows = ref[SLOTS : SLOTS + MARK, :128].astype(F32)
    return rows[:1, : TAIL + SPARE].astype(jnp.int32)


def merge_rows(len_ref, rest_ref, got_ref, out_ref):
    rest, got = rest_ref[...], got_ref[:SLOTS, :]
    out_ref[:TAIL, :] = merged(rest[:TAIL], got[CAP:], live(len_ref))
    out_ref[TAIL : TAIL + HEAD, :] = got[:HEAD]
    out_ref[TAIL + HEAD :, :] = merged(got[HEAD:CAP], rest[TAIL:], other_count(got_ref))


def order_token(after_ref, out_ref):
    out_ref[...] = jnp.zeros_like(out_ref)


def merge_cot(len_ref, own_ref, got_ref, after_ref, cot_out):
    own, got = own_ref[:SLOTS, :], got_ref[:SLOTS, :]
    cot_out[:HEAD, :] = own[:HEAD]
    cot_out[HEAD:CAP, :] = merged(own[HEAD:CAP], got[CAP:], live(len_ref))
    cot_out[CAP : CAP + HEAD, :] = got[:HEAD]
    cot_out[CAP + HEAD :, :] = merged(got[HEAD:CAP], own[CAP:], other_count(got_ref))


def near_terms(head_ref, tail_ref, far_head_ref, cot_ref, wide_ref, down_ref, sum_out):
    rows = jnp.concatenate([head_ref[...], tail_ref[...], far_head_ref[...]], axis=0)
    sum_out[:, : 2 * UP] = mm(rows, wide_ref[...], ((1,), (1,)))
    sum_out[: 2 * CAP, 2 * UP : 2 * UP + HH] = mm(cot_ref[...], down_ref[...], ((1,), (1,)))
    sum_out[: 2 * CAP, 2 * UP + HH :] = jnp.zeros((2 * CAP, 128 - HH), F32)
    sum_out[2 * CAP :, 2 * UP :] = jnp.zeros((HEAD, 128), F32)


def next_back(cot_ref, down_ref, out_ref):
    out_ref[:, :HH] = mm(cot_ref[...], down_ref[...], ((1,), (1,))).astype(out_ref.dtype)
    out_ref[:, HH:] = jnp.zeros((2 * CAP, 128 - HH), out_ref.dtype)


def far_terms(tail_ref, wide_ref, back_ref, out_ref):
    out_ref[: CAP + TAIL] = mm(tail_ref[...], wide_ref[...], ((1,), (1,))).astype(out_ref.dtype)
    for k in range(4):
        out_ref[CAP + TAIL :, k * 128 : (k + 1) * 128] = back_ref[k * 64 : (k + 1) * 64, :]


def swapped(value):
    return jnp.concatenate([value[CAP:], value[:CAP]], axis=0)


def both_halves(core, mine, other):
    low, high = jnp.where(core == 0, mine, other), jnp.where(core == 0, other, mine)
    lane = lax.broadcasted_iota(jnp.int32, low.shape, 1)
    high = pltpu.roll(high, HH, 1)
    return jnp.concatenate([jnp.where(lane < HH, low, high), high], axis=1)[:, :HB]


def hidden_grads(gate, up, back):
    sig = jax.nn.sigmoid(gate)
    gate_back = back * up * sig * (1.0 + gate * (1.0 - sig))
    return gate_back.astype(BF), (back * (gate * sig)).astype(BF)


def near_grads(core_ref, mine_ref, other_ref, gate_out, up_out, early_out):
    mine, other = mine_ref[: 2 * CAP], swapped(other_ref[: 2 * CAP])
    total = mine[:, : 2 * UP] + other[:, : 2 * UP]
    back = both_halves(core_ref[0], mine[:, 2 * UP :], other[:, 2 * UP :])
    gate_out[...], up_out[...] = hidden_grads(total[:, :HB], total[:, UP : UP + HB], back)
    early_out[...] = jnp.zeros_like(early_out)
    early_out[:HEAD] = mine_ref[2 * CAP :, : 2 * UP]
    early_out[CAP : CAP + HEAD] = other_ref[2 * CAP :, : 2 * UP]


def weight_grads(
    core_ref, early_ref, mine_ref, other_ref, back_ref, gate_ref, up_ref,
    head_ref, tail_ref, far_head_ref, far_tail_ref, out_ref, gate_all, up_all,
):
    @pl.when(pl.program_id(0) == 0)
    def _():
        mine, other = mine_ref[...].astype(F32), other_ref[...].astype(F32)
        early = early_ref[...]
        total = jnp.concatenate(
            [
                early[:HEAD] + other[TAIL : TAIL + HEAD],
                mine[:TAIL] + other[TAIL + HEAD : CAP + TAIL],
                early[CAP : CAP + HEAD] + mine[TAIL : TAIL + HEAD],
                mine[TAIL + HEAD : CAP + TAIL] + other[:TAIL],
            ],
            axis=0,
        )
        cross = other[CAP + TAIL :]
        cross = jnp.concatenate([cross[:, k * 128 : (k + 1) * 128] for k in range(4)], axis=0)
        back = both_halves(core_ref[0], back_ref[...].astype(F32), swapped(cross))
        gate_all[2 * CAP :], up_all[2 * CAP :] = hidden_grads(
            total[:, :HB], total[:, UP : UP + HB], back
        )
        gate_all[: 2 * CAP] = gate_ref[...]
        up_all[: 2 * CAP] = up_ref[...]

    rows = jnp.concatenate(
        [head_ref[...], tail_ref[...], far_head_ref[...], far_tail_ref[...]], axis=0
    )
    each = HALF // FIRST
    for at, weights in ((0, gate_all), (HB, up_all)):
        total = mm(weights[...], rows, ((0,), (0,))).astype(BF)
        for k in range(ABREAST):
            out_ref[k, at : at + HB] = total[:, k * each : (k + 1) * each]


def first_sum(in_ref, out_ref):
    total = in_ref[0].astype(F32)
    for k in range(1, FIRST):
        total += in_ref[k].astype(F32)
    lane = lax.broadcasted_iota(jnp.int32, (HB, 128), 1)
    for k in range(SECOND // 2):
        gate = total[:HB, k * 128 : (k + 1) * 128]
        up = total[HB:, k * 128 : (k + 1) * 128]
        out_ref[2 * k] = jnp.where(lane < 64, gate, pltpu.roll(up, 64, 1)).astype(BF)
        out_ref[2 * k + 1] = jnp.where(lane < 64, pltpu.roll(gate, 64, 1), up).astype(BF)


def second_sum(in_ref, gate_out, up_out):
    total = in_ref[0].astype(F32)
    for k in range(1, SECOND):
        total += in_ref[k].astype(F32)
    full = jnp.concatenate([total, jnp.zeros((UP - HB, 128), F32)], axis=0).T
    gate_out[...] = full[:64, :HB]
    up_out[...] = full[64:, :HB]


def along_z(block, distance):
    n = lax.axis_size("z")
    return lax.ppermute(block, "z", [(i, (i + distance) % n) for i in range(n)])


def between_cores(block):
    return lax.ppermute(block, "c", [(0, 1), (1, 0)])


def on_device(tokens, cotangent, gate_weight, up_weight, down_weight, lengths, rewards):
    core = lax.axis_index("c").astype(jnp.int32).reshape(1)
    half = lax.dynamic_slice_in_dim(down_weight, lax.axis_index("c") * HH, HH, 0)
    next_half = along_z(half, -1)
    head, rest, row_other = call(
        split_rows,
        (shape(HEAD, HALF), shape(SLOTS - HEAD, HALF), shape(SLOTS + MARK, HALF)),
        in_specs=[SMEM, SMEM, VMEM], cost=1.7,
    )(core, lengths, tokens)
    far_head = along_z(head, 1)
    row_got = between_cores(row_other)
    tail = call(
        merge_rows, shape(CAP + TAIL, HALF), cost=0.01,
                in_specs=[SMEM, VMEM, VMEM],
    )(lengths, rest, row_got)
    far_tail = along_z(tail, 1)
    cot_own = call(
        weigh, shape(SLOTS + MARK, D), in_specs=[SMEM, SMEM, VMEM, ANY], cost=0.01,
    )(lengths, rewards, cotangent, tail)
    cot_got = between_cores(cot_own)

    token = call(
        order_token, shape(8, 128, kind=F32), cost=2.7, in_specs=[ANY],
    )(next_half)
    cot_rows = call(
        merge_cot, shape(2 * CAP, D), cost=1, in_specs=[SMEM] + [VMEM] * 2 + [ANY],
    )(lengths, cot_own, cot_got, token)
    back = call(
        next_back, shape(2 * CAP, 128), cost=0.5,
        in_specs=[VMEM] * 2,
    )(cot_rows, next_half)
    far_back = along_z(back, 1)
    wide = call(
        split_wide, shape(2 * UP, HALF), in_specs=[SMEM, VMEM, VMEM, ANY], cost=0.01,
    )(core, gate_weight.T, up_weight.T, back)
    near = call(
        near_terms, shape(2 * CAP + HEAD, 2 * UP + 128, kind=F32),
        cost=0.01, in_specs=[VMEM] * 6,
    )(head, tail, far_head, cot_rows, wide, half)
    near_other = between_cores(near)
    gate_near, up_near, early = call(
        near_grads,
        (shape(2 * CAP, HB), shape(2 * CAP, HB), shape(2 * CAP, 2 * UP, kind=F32)),
        cost=0.3, in_specs=[SMEM] + [VMEM] * 2,
    )(core, near, near_other)
    far = call(
        far_terms, shape(CAP + TAIL + 64, 2 * UP), cost=10, in_specs=[VMEM] * 3
    )(far_tail, wide, far_back)
    far_other = between_cores(far)

    each = HALF // FIRST
    whole = lambda *dims: pl.BlockSpec(dims, lambda i: (0,) * len(dims))
    part = lambda rows: pl.BlockSpec((rows, ABREAST * each), lambda i: (0, i))
    grads = call(
        weight_grads, shape(FIRST, 2 * HB, each),
        scratch=[pltpu.VMEM((4 * CAP, HB), BF)] * 2, cost=2.1,
        grid=(FIRST // ABREAST,),
        in_specs=[SMEM, whole(2 * CAP, 2 * UP)] + [whole(CAP + TAIL + 64, 2 * UP)] * 2
        + [whole(2 * CAP, 128)] + [whole(2 * CAP, HB)] * 2
        + [part(HEAD), part(CAP + TAIL)] * 2,
        out_specs=pl.BlockSpec((ABREAST, 2 * HB, each), lambda i: (i, 0, 0)),
    )(core, early, far, far_other, far_back, gate_near, up_near, head, tail, far_head, far_tail)
    grads = lax.all_to_all(grads, ("xh", "xl", "yl"), split_axis=0, concat_axis=0, tiled=True)
    grads = call(
        first_sum, shape(SECOND, HB, 128), cost=0.4,
    )(grads)
    grads = lax.all_to_all(grads, "yh", split_axis=0, concat_axis=0, tiled=True)
    return call(
        second_sum, (shape(64, HB, kind=F32), shape(64, HB, kind=F32)),
                in_specs=[VMEM],
    )(grads)


def solution(mesh):
    planes = mesh.shape["blk"]
    names = ("z", "xl", "yh", "yl", "xh", "c")
    fine = Mesh(mesh.devices.reshape(planes, 2, 4, 2, 2, 2), names)
    rows = P(names, None)
    placed = (rows, rows, P(None, "z"), P(None, "z"), P("z", None), rows, rows)
    out = P(names[1:], "z")
    return jax.shard_map(
        on_device, mesh=fine, in_specs=placed, out_specs=(out, out), check_vma=False
    )
```

```python
import functools

import jax
import jax.numpy as jnp
from jax import lax
from jax.experimental import pallas as pl
from jax.experimental.pallas import tpu as pltpu
from jax.sharding import Mesh
from jax.sharding import PartitionSpec as P

D = 4096
HALF = D // 2
HB = 224
SLOTS = 160
CAP = 128
HEAD = 96
TAIL = CAP - HEAD
SPARE = SLOTS - CAP
FAR = HEAD + 2 * TAIL
UP = 256
MARK = 16
HH = HB // 2
FIRST, SECOND = 8, 4
ABREAST = 2
BF, F32 = jnp.bfloat16, jnp.float32
VMEM = pl.BlockSpec(memory_space=pltpu.VMEM)
SMEM = pl.BlockSpec(memory_space=pltpu.SMEM)
ANY = pl.BlockSpec(memory_space=pl.ANY)


def source_tile(first, second):
    x_hi, x_lo, y = first // 4, first // 2 % 2, 2 * second + first % 2
    return (x_lo * 8 + y) * 2 + x_hi


def call(body, outs, scratch=(), room=32, cost=0.0, **more):
    return pl.pallas_call(
        body,
        out_shape=outs,
        scratch_shapes=scratch,
        cost_estimate=pl.CostEstimate(flops=int(cost * 1e10), bytes_accessed=int(cost * 1e6), transcendentals=0),
        compiler_params=pltpu.CompilerParams(vmem_limit_bytes=room * 1024 * 1024),
        **more,
    )


def shape(*dims, kind=BF):
    return jax.ShapeDtypeStruct(dims, kind)


def mm(a, b, dims=((1,), (0,))):
    return lax.dot_general(a, b, (dims, ((), ())), preferred_element_type=F32)


def sorter(core):
    src = lax.broadcasted_iota(jnp.int32, (256, 256), 0)
    dst = lax.broadcasted_iota(jnp.int32, (256, 256), 1)
    lane = dst % 128
    side = jnp.where(dst < 128, core, 1 - core)
    want = (lane // 64) * 128 + side * 64 + lane % 64
    return jnp.where(src == want, 1.0, 0.0).astype(BF)


def sorted_tiles(ref, perm):
    for k in range(HALF // 128):
        first, second = (2 * k) // SECOND, (2 * k) % SECOND
        both = [
            ref[:, t * 128 : (t + 1) * 128]
            for t in (source_tile(first, second), source_tile(first, second + 1))
        ]
        yield slice(k * 128, (k + 1) * 128), mm(jnp.concatenate(both, axis=1), perm).astype(BF)


def mark(len_ref, columns):
    return jnp.full((MARK, columns), live(len_ref), jnp.int32).astype(F32).astype(BF)


def live(len_ref):
    return len_ref[0, 0] + len_ref[0, 1] + len_ref[0, 2] + len_ref[0, 3]


def take_head(tok_ref, after_ref, out_ref):
    out_ref[...] = tok_ref[:HEAD, :]


def split_rows(core_ref, len_ref, tok_ref, own_out, other_out):
    other_out[SLOTS:, :] = mark(len_ref, HALF)
    for at, tile in sorted_tiles(tok_ref, sorter(core_ref[0])):
        own_out[:, at] = tile[:, :128]
        other_out[:SLOTS, at] = tile[:, 128:]


def split_far(core_ref, row_ref, after_ref, own_out, other_out):
    for at, tile in sorted_tiles(row_ref, sorter(core_ref[0])):
        own_out[:, at] = tile[:, :128]
        other_out[:, at] = tile[:, 128:]


def split_wide(core_ref, gate_ref, up_ref, after_ref, wide_out):
    perm = sorter(core_ref[0])
    wide_out[HB:UP, :] = jnp.zeros((UP - HB, HALF), BF)
    wide_out[UP + HB :, :] = jnp.zeros((UP - HB, HALF), BF)
    for at, tile in sorted_tiles(gate_ref, perm):
        wide_out[:HB, at] = tile[:, :128]
    for at, tile in sorted_tiles(up_ref, perm):
        wide_out[UP : UP + HB, at] = tile[:, :128]


def weigh(len_ref, rew_ref, cot_ref, after_ref, out_ref):
    row = lax.broadcasted_iota(jnp.int32, (SLOTS, 1), 0)
    weight, start = jnp.zeros((SLOTS, 1), F32), jnp.int32(0)
    for j in range(4):
        end = start + len_ref[0, j]
        scaled = jnp.full((SLOTS, 1), rew_ref[0, j], jnp.int32).astype(F32) / 65536.0
        weight += jnp.where((row >= start) & (row < end), scaled, 0.0)
        start = end
    out_ref[:SLOTS, :] = (weight * cot_ref[...].astype(F32)).astype(BF)
    out_ref[SLOTS:, :] = mark(len_ref, D)


def merged(tail, surplus, count):
    slot = lax.broadcasted_iota(jnp.int32, (TAIL, TAIL + SPARE), 0)
    src = lax.broadcasted_iota(jnp.int32, (TAIL, TAIL + SPARE), 1)
    want = jnp.where(HEAD + slot < count, slot, TAIL + slot - jnp.maximum(count - HEAD, 0))
    pick = jnp.where(src == want, 1.0, 0.0).astype(BF)
    return mm(pick, jnp.concatenate([tail, surplus], axis=0)).astype(BF)


def other_count(ref):
    rows = ref[SLOTS : SLOTS + MARK, :128].astype(F32)
    return rows[:1, : TAIL + SPARE].astype(jnp.int32)


def merge_rows(len_ref, own_ref, got_ref, row_out, tail_out):
    own, got = own_ref[...], got_ref[:SLOTS, :]
    tail_out[:TAIL, :] = merged(own[HEAD:CAP], got[CAP:], live(len_ref))
    tail_out[TAIL:, :] = merged(got[HEAD:CAP], own[CAP:], other_count(got_ref))
    row_out[:HEAD, :] = own[:HEAD]
    row_out[HEAD:CAP, :] = tail_out[:TAIL, :]
    row_out[CAP : CAP + HEAD, :] = got[:HEAD]
    row_out[CAP + HEAD :, :] = tail_out[TAIL:, :]


def order_token(after_ref, behind_ref, out_ref):
    out_ref[...] = jnp.zeros_like(out_ref)


def near_terms(row_ref, wide_ref, sum_out):
    sum_out[...] = mm(row_ref[...], wide_ref[...], ((1,), (1,)))


def next_back(len_ref, own_ref, got_ref, next_ref, after_ref, behind_ref, cot_out, back_out):
    own, got, weights = own_ref[:SLOTS, :], got_ref[:SLOTS, :], next_ref[...]
    own_tail = merged(own[HEAD:CAP], got[CAP:], live(len_ref))
    got_tail = merged(got[HEAD:CAP], own[CAP:], other_count(got_ref))
    back_out[:, HH:] = jnp.zeros((2 * CAP, 128 - HH), BF)
    at = 0
    for part in (own[:HEAD], own_tail, got[:HEAD], got_tail):
        here = slice(at, at + part.shape[0])
        back_out[here, :HH] = mm(part, weights, ((1,), (1,))).astype(BF)
        at += part.shape[0]
    cot_out[:TAIL, :] = own_tail
    cot_out[TAIL:, :] = got_tail


def near_back(own_ref, got_ref, tail_ref, down_ref, after_ref, back_out):
    tail = tail_ref[...]
    parts = (own_ref[:HEAD, :], tail[:TAIL], got_ref[:HEAD, :], tail[TAIL:])
    back_out[:, HH:] = jnp.zeros((2 * CAP, 128 - HH), BF)
    cot = jnp.concatenate(parts, axis=0)
    back_out[:, :HH] = mm(cot, down_ref[...], ((1,), (1,))).astype(BF)


def far_rows(own_ref, got_ref, tail_ref):
    tail = tail_ref[...]
    return jnp.concatenate([own_ref[...], tail[:TAIL], got_ref[...], tail[TAIL:]], axis=0)


def far_terms(head_ref, gate_ref, up_ref, tail_ref, wide_ref, back_ref, near_ref, out_ref):
    out_ref[:HEAD, :] = jnp.zeros((HEAD, 2 * UP), BF)
    head = head_ref[...]
    out_ref[:HEAD, :HB] = mm(head, gate_ref[...], ((1,), (1,))).astype(BF)
    out_ref[:HEAD, UP : UP + HB] = mm(head, up_ref[...], ((1,), (1,))).astype(BF)
    out_ref[HEAD:FAR] = mm(tail_ref[...], wide_ref[...], ((1,), (1,))).astype(BF)
    for at, ref in ((FAR, back_ref), (FAR + 64, near_ref)):
        for k in range(4):
            out_ref[at : at + 64, k * 128 : (k + 1) * 128] = ref[k * 64 : (k + 1) * 64, :]


def swapped(value):
    return jnp.concatenate([value[CAP:], value[:CAP]], axis=0)


def both_halves(core, mine, other):
    low, high = jnp.where(core == 0, mine, other), jnp.where(core == 0, other, mine)
    lane = lax.broadcasted_iota(jnp.int32, low.shape, 1)
    high = pltpu.roll(high, HH, 1)
    return jnp.concatenate([jnp.where(lane < HH, low, high), high], axis=1)[:, :HB]


def hidden_grads(gate, up, back):
    sig = jax.nn.sigmoid(gate)
    gate_back = back * up * sig * (1.0 + gate * (1.0 - sig))
    return gate_back.astype(BF), (back * (gate * sig)).astype(BF)


def weight_grads(
    core_ref, near_ref, near_got_ref, mine_ref, other_ref, back_ref, near_back_ref,
    row_ref, far_own_ref, far_got_ref, far_tail_ref, out_ref, gate_all, up_all,
):
    def one(start, total, back, packed):
        cross = jnp.concatenate([packed[:, k * 128 : (k + 1) * 128] for k in range(4)], axis=0)
        back = both_halves(core_ref[0], back.astype(F32), swapped(cross.astype(F32)))
        at = slice(start, start + 2 * CAP)
        gate_all[at], up_all[at] = hidden_grads(total[:, :HB], total[:, UP : UP + HB], back)

    @pl.when(pl.program_id(0) == 0)
    def _():
        near = near_ref[...] + swapped(near_got_ref[...])
        one(0, near, near_back_ref[...], other_ref[FAR + 64 :, :])
        mine, other = mine_ref[:FAR, :].astype(F32), other_ref[:FAR, :].astype(F32)
        far = jnp.concatenate(
            [
                mine[:HEAD],
                mine[HEAD:CAP] + other[CAP:],
                other[:HEAD],
                mine[CAP:] + other[HEAD:CAP],
            ],
            axis=0,
        )
        one(2 * CAP, far, back_ref[...], other_ref[FAR : FAR + 64, :])

    rows = jnp.concatenate([row_ref[...], far_rows(far_own_ref, far_got_ref, far_tail_ref)], axis=0)
    each = HALF // FIRST
    for k in range(ABREAST):
        at = slice(k * each, (k + 1) * each)
        out_ref[k, :HB] = mm(gate_all[...], rows[:, at], ((0,), (0,))).astype(BF)
        out_ref[k, HB:] = mm(up_all[...], rows[:, at], ((0,), (0,))).astype(BF)


def first_sum(in_ref, out_ref):
    total = in_ref[0].astype(F32)
    for k in range(1, FIRST):
        total += in_ref[k].astype(F32)
    lane = lax.broadcasted_iota(jnp.int32, (HB, 128), 1)
    for k in range(SECOND // 2):
        gate = total[:HB, k * 128 : (k + 1) * 128]
        up = total[HB:, k * 128 : (k + 1) * 128]
        out_ref[2 * k] = jnp.where(lane < 64, gate, pltpu.roll(up, 64, 1)).astype(BF)
        out_ref[2 * k + 1] = jnp.where(lane < 64, pltpu.roll(gate, 64, 1), up).astype(BF)


def second_sum(in_ref, gate_out, up_out):
    total = in_ref[0].astype(F32)
    for k in range(1, SECOND):
        total += in_ref[k].astype(F32)
    full = jnp.concatenate([total, jnp.zeros((UP - HB, 128), F32)], axis=0).T
    gate_out[...] = full[:64, :HB]
    up_out[...] = full[64:, :HB]


def along_z(block, distance):
    n = lax.axis_size("z")
    return lax.ppermute(block, "z", [(i, (i + distance) % n) for i in range(n)])


def between_cores(block):
    return lax.ppermute(block, "c", [(0, 1), (1, 0)])


def on_device(tokens, cotangent, gate_weight, up_weight, down_weight, lengths, rewards):
    core = lax.axis_index("c").astype(jnp.int32).reshape(1)
    half = lax.dynamic_slice_in_dim(down_weight, lax.axis_index("c") * HH, HH, 0)
    next_half = along_z(half, -1)
    head = call(
        take_head, shape(HEAD, D), cost=0.01, in_specs=[VMEM, ANY],
    )(tokens, half)
    far_head = along_z(head, 1)
    own, other = call(
        split_rows, (shape(SLOTS, HALF), shape(SLOTS + MARK, HALF)),
        in_specs=[SMEM, SMEM, VMEM], cost=1.7,
    )(core, lengths, tokens)
    row_got = between_cores(other)
    rows, tail = call(
        merge_rows, (shape(2 * CAP, HALF), shape(2 * TAIL, HALF)), cost=0.01,
        in_specs=[SMEM, VMEM, VMEM],
    )(lengths, own, row_got)
    far_tail = along_z(tail, 1)
    cot_own = call(
        weigh, shape(SLOTS + MARK, D), in_specs=[SMEM, SMEM, VMEM, ANY], cost=0.01,
    )(lengths, rewards, cotangent, tail)
    cot_got = between_cores(cot_own)

    wide = call(
        split_wide, shape(2 * UP, HALF), in_specs=[SMEM, VMEM, VMEM, ANY], cost=0.01,
    )(core, gate_weight.T, up_weight.T, cot_own)
    near = call(
        near_terms, shape(2 * CAP, 2 * UP, kind=F32), cost=0.01, in_specs=[VMEM] * 2,
    )(rows, wide)
    near_got = between_cores(near)
    token = call(
        order_token, shape(8, 128, kind=F32), cost=2.7, in_specs=[ANY, ANY],
    )(next_half, far_head)
    cot_tail, back = call(
        next_back, (shape(2 * TAIL, D), shape(2 * CAP, 128)), cost=1.5,
        in_specs=[SMEM] + [VMEM] * 3 + [ANY, ANY],
    )(lengths, cot_own, cot_got, next_half, token, near_got)
    far_back = along_z(back, 1)
    back_near = call(
        near_back, shape(2 * CAP, 128), cost=0.01, in_specs=[VMEM] * 4 + [ANY],
    )(cot_own, cot_got, cot_tail, half, back)
    far_own, far_other_half = call(
        split_far, (shape(HEAD, HALF), shape(HEAD, HALF)), cost=0.01, in_specs=[SMEM, VMEM, ANY],
    )(core, far_head, back)
    far_got = between_cores(far_other_half)
    far = call(
        far_terms, shape(FAR + 128, 2 * UP), cost=10, in_specs=[VMEM] * 7
    )(far_head, gate_weight.T, up_weight.T, far_tail, wide, far_back, back_near)
    far_other = between_cores(far)

    each = HALF // FIRST
    whole = lambda *dims: pl.BlockSpec(dims, lambda i: (0,) * len(dims))
    part = lambda rows: pl.BlockSpec((rows, ABREAST * each), lambda i: (0, i))
    grads = call(
        weight_grads, shape(FIRST, 2 * HB, each),
        scratch=[pltpu.VMEM((4 * CAP, HB), BF)] * 2, cost=2.1,
        grid=(FIRST // ABREAST,),
        in_specs=[SMEM] + [whole(2 * CAP, 2 * UP)] * 2 + [whole(FAR + 128, 2 * UP)] * 2
        + [whole(2 * CAP, 128)] * 2
        + [part(2 * CAP), part(HEAD), part(HEAD), part(2 * TAIL)],
        out_specs=pl.BlockSpec((ABREAST, 2 * HB, each), lambda i: (i, 0, 0)),
    )(
        core, near, near_got, far, far_other, far_back, back_near,
        rows, far_own, far_got, far_tail,
    )
    grads = lax.all_to_all(grads, ("xh", "xl", "yl"), split_axis=0, concat_axis=0, tiled=True)
    grads = call(
        first_sum, shape(SECOND, HB, 128), cost=0.4,
    )(grads)
    grads = lax.all_to_all(grads, "yh", split_axis=0, concat_axis=0, tiled=True)
    return call(
        second_sum, (shape(64, HB, kind=F32), shape(64, HB, kind=F32)),
                in_specs=[VMEM],
    )(grads)


def solution(mesh):
    planes = mesh.shape["blk"]
    names = ("z", "xl", "yh", "yl", "xh", "c")
    fine = Mesh(mesh.devices.reshape(planes, 2, 4, 2, 2, 2), names)
    rows = P(names, None)
    placed = (rows, rows, P(None, "z"), P(None, "z"), P("z", None), rows, rows)
    out = P(names[1:], "z")
    return jax.shard_map(
        on_device, mesh=fine, in_specs=placed, out_specs=(out, out), check_vma=False
    )
```

```python
import functools

import jax
import jax.numpy as jnp
from jax import lax
from jax.experimental import pallas as pl
from jax.experimental.pallas import tpu as pltpu
from jax.sharding import Mesh
from jax.sharding import PartitionSpec as P

D = 4096
HALF = D // 2
HB = 224
SLOTS = 160
CAP = 128
HEAD = 96
TAIL = CAP - HEAD
SPARE = SLOTS - CAP
UP = 256
MARK = 16
HH = HB // 2
FIRST, SECOND = 8, 4
ABREAST = 2
BF, F32 = jnp.bfloat16, jnp.float32
VMEM = pl.BlockSpec(memory_space=pltpu.VMEM)
SMEM = pl.BlockSpec(memory_space=pltpu.SMEM)
ANY = pl.BlockSpec(memory_space=pl.ANY)


def source_tile(first, second):
    x_hi, x_lo, y = first // 4, first // 2 % 2, 2 * second + first % 2
    return (x_lo * 8 + y) * 2 + x_hi


def call(body, outs, scratch=(), room=32, cost=0.0, **more):
    return pl.pallas_call(
        body,
        out_shape=outs,
        scratch_shapes=scratch,
        cost_estimate=pl.CostEstimate(flops=int(cost * 1e10), bytes_accessed=int(cost * 1e6), transcendentals=0),
        compiler_params=pltpu.CompilerParams(vmem_limit_bytes=room * 1024 * 1024),
        **more,
    )


def shape(*dims, kind=BF):
    return jax.ShapeDtypeStruct(dims, kind)


def mm(a, b, dims=((1,), (0,))):
    return lax.dot_general(a, b, (dims, ((), ())), preferred_element_type=F32)


def sorter(core):
    src = lax.broadcasted_iota(jnp.int32, (256, 256), 0)
    dst = lax.broadcasted_iota(jnp.int32, (256, 256), 1)
    lane = dst % 128
    side = jnp.where(dst < 128, core, 1 - core)
    want = (lane // 64) * 128 + side * 64 + lane % 64
    return jnp.where(src == want, 1.0, 0.0).astype(BF)


def sorted_tiles(ref, perm):
    for k in range(HALF // 128):
        first, second = (2 * k) // SECOND, (2 * k) % SECOND
        both = [
            ref[:, t * 128 : (t + 1) * 128]
            for t in (source_tile(first, second), source_tile(first, second + 1))
        ]
        yield slice(k * 128, (k + 1) * 128), mm(jnp.concatenate(both, axis=1), perm).astype(BF)


def mark(len_ref, columns):
    return jnp.full((MARK, columns), live(len_ref), jnp.int32).astype(F32).astype(BF)


def live(len_ref):
    return len_ref[0, 0] + len_ref[0, 1] + len_ref[0, 2] + len_ref[0, 3]


def split_rows(core_ref, len_ref, tok_ref, head_out, rest_out, other_out):
    perm = sorter(core_ref[0])
    other_out[SLOTS:, :] = mark(len_ref, HALF)
    for at, tile in sorted_tiles(tok_ref, perm):
        head_out[:, at] = tile[:HEAD, :128]
        rest_out[:, at] = tile[HEAD:, :128]
        other_out[:SLOTS, at] = tile[:, 128:]


def split_wide(core_ref, gate_ref, up_ref, after_ref, wide_out):
    perm = sorter(core_ref[0])
    wide_out[HB:UP, :] = jnp.zeros((UP - HB, HALF), BF)
    wide_out[UP + HB :, :] = jnp.zeros((UP - HB, HALF), BF)
    for at, tile in sorted_tiles(gate_ref, perm):
        wide_out[:HB, at] = tile[:, :128]
    for at, tile in sorted_tiles(up_ref, perm):
        wide_out[UP : UP + HB, at] = tile[:, :128]


def weigh(len_ref, rew_ref, cot_ref, after_ref, out_ref):
    row = lax.broadcasted_iota(jnp.int32, (SLOTS, 1), 0)
    weight, start = jnp.zeros((SLOTS, 1), F32), jnp.int32(0)
    for j in range(4):
        end = start + len_ref[0, j]
        scaled = jnp.full((SLOTS, 1), rew_ref[0, j], jnp.int32).astype(F32) / 65536.0
        weight += jnp.where((row >= start) & (row < end), scaled, 0.0)
        start = end
    out_ref[:SLOTS, :] = (weight * cot_ref[...].astype(F32)).astype(BF)
    out_ref[SLOTS:, :] = mark(len_ref, D)


def merged(tail, surplus, count):
    slot = lax.broadcasted_iota(jnp.int32, (TAIL, TAIL + SPARE), 0)
    src = lax.broadcasted_iota(jnp.int32, (TAIL, TAIL + SPARE), 1)
    want = jnp.where(HEAD + slot < count, slot, TAIL + slot - jnp.maximum(count - HEAD, 0))
    pick = jnp.where(src == want, 1.0, 0.0).astype(BF)
    return mm(pick, jnp.concatenate([tail, surplus], axis=0)).astype(BF)


def other_count(ref):
    rows = ref[SLOTS : SLOTS + MARK, :128].astype(F32)
    return rows[:1, : TAIL + SPARE].astype(jnp.int32)


def merge_rows(len_ref, rest_ref, got_ref, out_ref):
    rest, got = rest_ref[...], got_ref[:SLOTS, :]
    out_ref[:TAIL, :] = merged(rest[:TAIL], got[CAP:], live(len_ref))
    out_ref[TAIL : TAIL + HEAD, :] = got[:HEAD]
    out_ref[TAIL + HEAD :, :] = merged(got[HEAD:CAP], rest[TAIL:], other_count(got_ref))


def order_token(after_ref, out_ref):
    out_ref[...] = jnp.zeros_like(out_ref)


def near_terms(
    head_ref, tail_ref, far_head_ref, own_ref, got_ref, cot_ref, wide_ref, down_ref, sum_out
):
    parts = (own_ref[:HEAD, :], cot_ref[:TAIL, :], got_ref[:HEAD, :], cot_ref[TAIL:, :])
    cot = jnp.concatenate(parts, axis=0)
    rows = jnp.concatenate([head_ref[...], tail_ref[...], far_head_ref[...]], axis=0)
    sum_out[:, : 2 * UP] = mm(rows, wide_ref[...], ((1,), (1,)))
    sum_out[: 2 * CAP, 2 * UP : 2 * UP + HH] = mm(cot, down_ref[...], ((1,), (1,)))
    sum_out[: 2 * CAP, 2 * UP + HH :] = jnp.zeros((2 * CAP, 128 - HH), F32)
    sum_out[2 * CAP :, 2 * UP :] = jnp.zeros((HEAD, 128), F32)


def next_back(len_ref, own_ref, got_ref, next_ref, after_ref, cot_out, back_out):
    own, got, weights = own_ref[:SLOTS, :], got_ref[:SLOTS, :], next_ref[...]
    own_tail = merged(own[HEAD:CAP], got[CAP:], live(len_ref))
    got_tail = merged(got[HEAD:CAP], own[CAP:], other_count(got_ref))
    back_out[:, HH:] = jnp.zeros((2 * CAP, 128 - HH), BF)
    cot = jnp.concatenate([own[:HEAD], own_tail, got[:HEAD], got_tail], axis=0)
    back_out[:, :HH] = mm(cot, weights, ((1,), (1,))).astype(BF)
    cot_out[:TAIL, :] = own_tail
    cot_out[TAIL:, :] = got_tail


def far_terms(tail_ref, wide_ref, back_ref, out_ref):
    out_ref[: CAP + TAIL] = mm(tail_ref[...], wide_ref[...], ((1,), (1,))).astype(out_ref.dtype)
    for k in range(4):
        out_ref[CAP + TAIL :, k * 128 : (k + 1) * 128] = back_ref[k * 64 : (k + 1) * 64, :]


def swapped(value):
    return jnp.concatenate([value[CAP:], value[:CAP]], axis=0)


def both_halves(core, mine, other):
    low, high = jnp.where(core == 0, mine, other), jnp.where(core == 0, other, mine)
    lane = lax.broadcasted_iota(jnp.int32, low.shape, 1)
    high = pltpu.roll(high, HH, 1)
    return jnp.concatenate([jnp.where(lane < HH, low, high), high], axis=1)[:, :HB]


def hidden_grads(gate, up, back):
    sig = jax.nn.sigmoid(gate)
    gate_back = back * up * sig * (1.0 + gate * (1.0 - sig))
    return gate_back.astype(BF), (back * (gate * sig)).astype(BF)


def near_grads(core_ref, mine_ref, other_ref, gate_out, up_out, early_out):
    mine, other = mine_ref[: 2 * CAP], swapped(other_ref[: 2 * CAP])
    total = mine[:, : 2 * UP] + other[:, : 2 * UP]
    back = both_halves(core_ref[0], mine[:, 2 * UP :], other[:, 2 * UP :])
    gate_out[...], up_out[...] = hidden_grads(total[:, :HB], total[:, UP : UP + HB], back)
    early_out[...] = jnp.zeros_like(early_out)
    early_out[:HEAD] = mine_ref[2 * CAP :, : 2 * UP]
    early_out[CAP : CAP + HEAD] = other_ref[2 * CAP :, : 2 * UP]


def weight_grads(
    core_ref, early_ref, mine_ref, other_ref, back_ref, gate_ref, up_ref,
    head_ref, tail_ref, far_head_ref, far_tail_ref, out_ref,
):
    mine, other = mine_ref[...].astype(F32), other_ref[...].astype(F32)
    early = early_ref[...]
    total = jnp.concatenate(
        [
            early[:HEAD] + other[TAIL : TAIL + HEAD],
            mine[:TAIL] + other[TAIL + HEAD : CAP + TAIL],
            early[CAP : CAP + HEAD] + mine[TAIL : TAIL + HEAD],
            mine[TAIL + HEAD : CAP + TAIL] + other[:TAIL],
        ],
        axis=0,
    )
    cross = other[CAP + TAIL :]
    cross = jnp.concatenate([cross[:, k * 128 : (k + 1) * 128] for k in range(4)], axis=0)
    back = both_halves(core_ref[0], back_ref[...].astype(F32), swapped(cross))
    gate, up = hidden_grads(total[:, :HB], total[:, UP : UP + HB], back)
    gate = jnp.concatenate([gate_ref[...], gate], axis=0)
    up = jnp.concatenate([up_ref[...], up], axis=0)
    each, parts = HALF // FIRST, (head_ref, tail_ref, far_head_ref, far_tail_ref)
    for k in range(0, FIRST, ABREAST):
        columns = slice(k * each, (k + ABREAST) * each)
        rows = jnp.concatenate([ref[:, columns] for ref in parts], axis=0)
        for at, weights in ((0, gate), (HB, up)):
            grads = mm(weights, rows, ((0,), (0,))).astype(BF)
            for m in range(ABREAST):
                out_ref[k + m, at : at + HB] = grads[:, m * each : (m + 1) * each]


def first_sum(in_ref, out_ref):
    total = in_ref[0].astype(F32)
    for k in range(1, FIRST):
        total += in_ref[k].astype(F32)
    lane = lax.broadcasted_iota(jnp.int32, (HB, 128), 1)
    for k in range(SECOND // 2):
        gate = total[:HB, k * 128 : (k + 1) * 128]
        up = total[HB:, k * 128 : (k + 1) * 128]
        out_ref[2 * k] = jnp.where(lane < 64, gate, pltpu.roll(up, 64, 1)).astype(BF)
        out_ref[2 * k + 1] = jnp.where(lane < 64, pltpu.roll(gate, 64, 1), up).astype(BF)


def second_sum(in_ref, gate_out, up_out):
    total = in_ref[0].astype(F32)
    for k in range(1, SECOND):
        total += in_ref[k].astype(F32)
    full = jnp.concatenate([total, jnp.zeros((UP - HB, 128), F32)], axis=0).T
    gate_out[...] = full[:64, :HB]
    up_out[...] = full[64:, :HB]


def along_z(block, distance):
    n = lax.axis_size("z")
    return lax.ppermute(block, "z", [(i, (i + distance) % n) for i in range(n)])


def between_cores(block):
    return lax.ppermute(block, "c", [(0, 1), (1, 0)])


def on_device(tokens, cotangent, gate_weight, up_weight, down_weight, lengths, rewards):
    core = lax.axis_index("c").astype(jnp.int32).reshape(1)
    half = lax.dynamic_slice_in_dim(down_weight, lax.axis_index("c") * HH, HH, 0)
    next_half = along_z(half, -1)
    head, rest, row_other = call(
        split_rows,
        (shape(HEAD, HALF), shape(SLOTS - HEAD, HALF), shape(SLOTS + MARK, HALF)),
        in_specs=[SMEM, SMEM, VMEM], cost=1.7,
    )(core, lengths, tokens)
    far_head = along_z(head, 1)
    row_got = between_cores(row_other)
    tail = call(
        merge_rows, shape(CAP + TAIL, HALF), cost=0.01,
                in_specs=[SMEM, VMEM, VMEM],
    )(lengths, rest, row_got)
    far_tail = along_z(tail, 1)
    cot_own = call(
        weigh, shape(SLOTS + MARK, D), in_specs=[SMEM, SMEM, VMEM, ANY], cost=0.01,
    )(lengths, rewards, cotangent, tail)
    cot_got = between_cores(cot_own)

    token = call(
        order_token, shape(8, 128, kind=F32), cost=2.7, in_specs=[ANY],
    )(next_half)
    cot_tail, back = call(
        next_back, (shape(2 * TAIL, D), shape(2 * CAP, 128)), cost=1.5,
        in_specs=[SMEM] + [VMEM] * 3 + [ANY],
    )(lengths, cot_own, cot_got, next_half, token)
    far_back = along_z(back, 1)
    wide = call(
        split_wide, shape(2 * UP, HALF), in_specs=[SMEM, VMEM, VMEM, ANY], cost=0.01,
    )(core, gate_weight.T, up_weight.T, back)
    near = call(
        near_terms, shape(2 * CAP + HEAD, 2 * UP + 128, kind=F32),
        cost=0.01, in_specs=[VMEM] * 8,
    )(head, tail, far_head, cot_own, cot_got, cot_tail, wide, half)
    near_other = between_cores(near)
    gate_near, up_near, early = call(
        near_grads,
        (shape(2 * CAP, HB), shape(2 * CAP, HB), shape(2 * CAP, 2 * UP, kind=F32)),
        cost=0.3, in_specs=[SMEM] + [VMEM] * 2,
    )(core, near, near_other)
    far = call(
        far_terms, shape(CAP + TAIL + 64, 2 * UP), cost=10, in_specs=[VMEM] * 3
    )(far_tail, wide, far_back)
    far_other = between_cores(far)

    grads = call(
        weight_grads, shape(FIRST, 2 * HB, HALF // FIRST), cost=2.1, in_specs=[SMEM] + [VMEM] * 10,
    )(core, early, far, far_other, far_back, gate_near, up_near, head, tail, far_head, far_tail)
    grads = lax.all_to_all(grads, ("xh", "xl", "yl"), split_axis=0, concat_axis=0, tiled=True)
    grads = call(
        first_sum, shape(SECOND, HB, 128), cost=0.4,
    )(grads)
    grads = lax.all_to_all(grads, "yh", split_axis=0, concat_axis=0, tiled=True)
    return call(
        second_sum, (shape(64, HB, kind=F32), shape(64, HB, kind=F32)),
                in_specs=[VMEM],
    )(grads)


def solution(mesh):
    planes = mesh.shape["blk"]
    names = ("z", "xl", "yh", "yl", "xh", "c")
    fine = Mesh(mesh.devices.reshape(planes, 2, 4, 2, 2, 2), names)
    rows = P(names, None)
    placed = (rows, rows, P(None, "z"), P(None, "z"), P("z", None), rows, rows)
    out = P(names[1:], "z")
    return jax.shard_map(
        on_device, mesh=fine, in_specs=placed, out_specs=(out, out), check_vma=False
    )
```

```python
import functools

import jax
import jax.numpy as jnp
from jax import lax
from jax.experimental import pallas as pl
from jax.experimental.pallas import tpu as pltpu
from jax.sharding import Mesh
from jax.sharding import PartitionSpec as P

D = 4096
HALF = D // 2
HB = 224
SLOTS = 160
CAP = 128
HEAD = 96
TAIL = CAP - HEAD
SPARE = SLOTS - CAP
UP = 256
MARK = 16
HH = HB // 2
FIRST, SECOND = 8, 4
ABREAST = 2
BF, F32 = jnp.bfloat16, jnp.float32
VMEM = pl.BlockSpec(memory_space=pltpu.VMEM)
SMEM = pl.BlockSpec(memory_space=pltpu.SMEM)
ANY = pl.BlockSpec(memory_space=pl.ANY)


def source_tile(first, second):
    x_hi, x_lo, y = first // 4, first // 2 % 2, 2 * second + first % 2
    return (x_lo * 8 + y) * 2 + x_hi


def call(body, outs, scratch=(), room=32, cost=0.0, **more):
    return pl.pallas_call(
        body,
        out_shape=outs,
        scratch_shapes=scratch,
        cost_estimate=pl.CostEstimate(flops=int(cost * 1e10), bytes_accessed=int(cost * 1e6), transcendentals=0),
        compiler_params=pltpu.CompilerParams(vmem_limit_bytes=room * 1024 * 1024),
        **more,
    )


def shape(*dims, kind=BF):
    return jax.ShapeDtypeStruct(dims, kind)


def mm(a, b, dims=((1,), (0,))):
    return lax.dot_general(a, b, (dims, ((), ())), preferred_element_type=F32)


def sorter(core):
    src = lax.broadcasted_iota(jnp.int32, (256, 256), 0)
    dst = lax.broadcasted_iota(jnp.int32, (256, 256), 1)
    lane = dst % 128
    side = jnp.where(dst < 128, core, 1 - core)
    want = (lane // 64) * 128 + side * 64 + lane % 64
    return jnp.where(src == want, 1.0, 0.0).astype(BF)


def sorted_tiles(ref, perm):
    for k in range(HALF // 128):
        first, second = (2 * k) // SECOND, (2 * k) % SECOND
        both = [
            ref[:, t * 128 : (t + 1) * 128]
            for t in (source_tile(first, second), source_tile(first, second + 1))
        ]
        yield slice(k * 128, (k + 1) * 128), mm(jnp.concatenate(both, axis=1), perm).astype(BF)


def mark(len_ref, columns):
    return jnp.full((MARK, columns), live(len_ref), jnp.int32).astype(F32).astype(BF)


def live(len_ref):
    return len_ref[0, 0] + len_ref[0, 1] + len_ref[0, 2] + len_ref[0, 3]


def split_rows(core_ref, len_ref, tok_ref, head_out, rest_out, other_out):
    perm = sorter(core_ref[0])
    other_out[SLOTS:, :] = mark(len_ref, HALF)
    for at, tile in sorted_tiles(tok_ref, perm):
        head_out[:, at] = tile[:HEAD, :128]
        rest_out[:, at] = tile[HEAD:, :128]
        other_out[:SLOTS, at] = tile[:, 128:]


def split_wide(core_ref, gate_ref, up_ref, after_ref, wide_out):
    perm = sorter(core_ref[0])
    wide_out[HB:UP, :] = jnp.zeros((UP - HB, HALF), BF)
    wide_out[UP + HB :, :] = jnp.zeros((UP - HB, HALF), BF)
    for at, tile in sorted_tiles(gate_ref, perm):
        wide_out[:HB, at] = tile[:, :128]
    for at, tile in sorted_tiles(up_ref, perm):
        wide_out[UP : UP + HB, at] = tile[:, :128]


def weigh(len_ref, rew_ref, cot_ref, after_ref, out_ref):
    row = lax.broadcasted_iota(jnp.int32, (SLOTS, 1), 0)
    weight, start = jnp.zeros((SLOTS, 1), F32), jnp.int32(0)
    for j in range(4):
        end = start + len_ref[0, j]
        scaled = jnp.full((SLOTS, 1), rew_ref[0, j], jnp.int32).astype(F32) / 65536.0
        weight += jnp.where((row >= start) & (row < end), scaled, 0.0)
        start = end
    out_ref[:SLOTS, :] = (weight * cot_ref[...].astype(F32)).astype(BF)
    out_ref[SLOTS:, :] = mark(len_ref, D)


def merged(tail, surplus, count):
    slot = lax.broadcasted_iota(jnp.int32, (TAIL, TAIL + SPARE), 0)
    src = lax.broadcasted_iota(jnp.int32, (TAIL, TAIL + SPARE), 1)
    want = jnp.where(HEAD + slot < count, slot, TAIL + slot - jnp.maximum(count - HEAD, 0))
    pick = jnp.where(src == want, 1.0, 0.0).astype(BF)
    return mm(pick, jnp.concatenate([tail, surplus], axis=0)).astype(BF)


def other_count(ref):
    rows = ref[SLOTS : SLOTS + MARK, :128].astype(F32)
    return rows[:1, : TAIL + SPARE].astype(jnp.int32)


def merge_rows(len_ref, rest_ref, got_ref, out_ref):
    rest, got = rest_ref[...], got_ref[:SLOTS, :]
    out_ref[:TAIL, :] = merged(rest[:TAIL], got[CAP:], live(len_ref))
    out_ref[TAIL : TAIL + HEAD, :] = got[:HEAD]
    out_ref[TAIL + HEAD :, :] = merged(got[HEAD:CAP], rest[TAIL:], other_count(got_ref))


def order_token(after_ref, out_ref):
    out_ref[...] = jnp.zeros_like(out_ref)


def near_terms(
    head_ref, tail_ref, far_head_ref, own_ref, got_ref, cot_ref, wide_ref, down_ref, sum_out
):
    parts = (own_ref[:HEAD, :], cot_ref[:TAIL, :], got_ref[:HEAD, :], cot_ref[TAIL:, :])
    cot = jnp.concatenate(parts, axis=0)
    rows = jnp.concatenate([head_ref[...], tail_ref[...], far_head_ref[...]], axis=0)
    sum_out[:, : 2 * UP] = mm(rows, wide_ref[...], ((1,), (1,)))
    sum_out[: 2 * CAP, 2 * UP : 2 * UP + HH] = mm(cot, down_ref[...], ((1,), (1,)))
    sum_out[: 2 * CAP, 2 * UP + HH :] = jnp.zeros((2 * CAP, 128 - HH), F32)
    sum_out[2 * CAP :, 2 * UP :] = jnp.zeros((HEAD, 128), F32)


def next_back(len_ref, own_ref, got_ref, next_ref, after_ref, cot_out, back_out):
    own, got, weights = own_ref[:SLOTS, :], got_ref[:SLOTS, :], next_ref[...]
    own_tail = merged(own[HEAD:CAP], got[CAP:], live(len_ref))
    got_tail = merged(got[HEAD:CAP], own[CAP:], other_count(got_ref))
    back_out[:, HH:] = jnp.zeros((2 * CAP, 128 - HH), BF)
    cot = jnp.concatenate([own[:HEAD], own_tail, got[:HEAD], got_tail], axis=0)
    back_out[:, :HH] = mm(cot, weights, ((1,), (1,))).astype(BF)
    cot_out[:TAIL, :] = own_tail
    cot_out[TAIL:, :] = got_tail


def far_terms(tail_ref, wide_ref, out_ref):
    out_ref[...] = mm(tail_ref[...], wide_ref[...], ((1,), (1,))).astype(out_ref.dtype)


def swapped(value):
    return jnp.concatenate([value[CAP:], value[:CAP]], axis=0)


def both_halves(core, mine, other):
    low, high = jnp.where(core == 0, mine, other), jnp.where(core == 0, other, mine)
    lane = lax.broadcasted_iota(jnp.int32, low.shape, 1)
    high = pltpu.roll(high, HH, 1)
    return jnp.concatenate([jnp.where(lane < HH, low, high), high], axis=1)[:, :HB]


def hidden_grads(gate, up, back):
    sig = jax.nn.sigmoid(gate)
    gate_back = back * up * sig * (1.0 + gate * (1.0 - sig))
    return gate_back.astype(BF), (back * (gate * sig)).astype(BF)


def near_grads(core_ref, mine_ref, other_ref, gate_out, up_out, early_out):
    mine, other = mine_ref[: 2 * CAP], swapped(other_ref[: 2 * CAP])
    total = mine[:, : 2 * UP] + other[:, : 2 * UP]
    back = both_halves(core_ref[0], mine[:, 2 * UP :], other[:, 2 * UP :])
    gate_out[...], up_out[...] = hidden_grads(total[:, :HB], total[:, UP : UP + HB], back)
    early_out[...] = jnp.zeros_like(early_out)
    early_out[:HEAD] = mine_ref[2 * CAP :, : 2 * UP]
    early_out[CAP : CAP + HEAD] = other_ref[2 * CAP :, : 2 * UP]


def weight_grads(
    core_ref, early_ref, mine_ref, other_ref, back_ref, cross_ref, gate_ref, up_ref,
    head_ref, tail_ref, far_head_ref, far_tail_ref, out_ref,
):
    mine, other = mine_ref[...].astype(F32), other_ref[...].astype(F32)
    early = early_ref[...]
    total = jnp.concatenate(
        [
            early[:HEAD] + other[TAIL : TAIL + HEAD],
            mine[:TAIL] + other[TAIL + HEAD : CAP + TAIL],
            early[CAP : CAP + HEAD] + mine[TAIL : TAIL + HEAD],
            mine[TAIL + HEAD : CAP + TAIL] + other[:TAIL],
        ],
        axis=0,
    )
    cross = swapped(cross_ref[...].astype(F32))
    back = both_halves(core_ref[0], back_ref[...].astype(F32), cross)
    gate, up = hidden_grads(total[:, :HB], total[:, UP : UP + HB], back)
    gate = jnp.concatenate([gate_ref[...], gate], axis=0)
    up = jnp.concatenate([up_ref[...], up], axis=0)
    each, parts = HALF // FIRST, (head_ref, tail_ref, far_head_ref, far_tail_ref)
    for k in range(0, FIRST, ABREAST):
        columns = slice(k * each, (k + ABREAST) * each)
        rows = jnp.concatenate([ref[:, columns] for ref in parts], axis=0)
        for at, weights in ((0, gate), (HB, up)):
            grads = mm(weights, rows, ((0,), (0,))).astype(BF)
            for m in range(ABREAST):
                out_ref[k + m, at : at + HB] = grads[:, m * each : (m + 1) * each]


def first_sum(in_ref, out_ref):
    total = in_ref[0].astype(F32)
    for k in range(1, FIRST):
        total += in_ref[k].astype(F32)
    lane = lax.broadcasted_iota(jnp.int32, (HB, 128), 1)
    for k in range(SECOND // 2):
        gate = total[:HB, k * 128 : (k + 1) * 128]
        up = total[HB:, k * 128 : (k + 1) * 128]
        out_ref[2 * k] = jnp.where(lane < 64, gate, pltpu.roll(up, 64, 1)).astype(BF)
        out_ref[2 * k + 1] = jnp.where(lane < 64, pltpu.roll(gate, 64, 1), up).astype(BF)


def second_sum(in_ref, gate_out, up_out):
    total = in_ref[0].astype(F32)
    for k in range(1, SECOND):
        total += in_ref[k].astype(F32)
    full = jnp.concatenate([total, jnp.zeros((UP - HB, 128), F32)], axis=0).T
    gate_out[...] = full[:64, :HB]
    up_out[...] = full[64:, :HB]


def along_z(block, distance):
    n = lax.axis_size("z")
    return lax.ppermute(block, "z", [(i, (i + distance) % n) for i in range(n)])


def along_z_crossed(block):
    n = lax.axis_size("z")
    route = [(2 * i + c, 2 * ((i + 1) % n) + 1 - c) for i in range(n) for c in range(2)]
    return lax.ppermute(block, ("z", "c"), route)


def between_cores(block):
    return lax.ppermute(block, "c", [(0, 1), (1, 0)])


def on_device(tokens, cotangent, gate_weight, up_weight, down_weight, lengths, rewards):
    core = lax.axis_index("c").astype(jnp.int32).reshape(1)
    half = lax.dynamic_slice_in_dim(down_weight, lax.axis_index("c") * HH, HH, 0)
    next_half = along_z(half, -1)
    head, rest, row_other = call(
        split_rows,
        (shape(HEAD, HALF), shape(SLOTS - HEAD, HALF), shape(SLOTS + MARK, HALF)),
        in_specs=[SMEM, SMEM, VMEM], cost=1.7,
    )(core, lengths, tokens)
    far_head = along_z(head, 1)
    row_got = between_cores(row_other)
    tail = call(
        merge_rows, shape(CAP + TAIL, HALF), cost=0.01,
                in_specs=[SMEM, VMEM, VMEM],
    )(lengths, rest, row_got)
    far_tail = along_z(tail, 1)
    cot_own = call(
        weigh, shape(SLOTS + MARK, D), in_specs=[SMEM, SMEM, VMEM, ANY], cost=0.01,
    )(lengths, rewards, cotangent, tail)
    cot_got = between_cores(cot_own)

    token = call(
        order_token, shape(8, 128, kind=F32), cost=2.7, in_specs=[ANY],
    )(next_half)
    cot_tail, back = call(
        next_back, (shape(2 * TAIL, D), shape(2 * CAP, 128)), cost=1.5,
        in_specs=[SMEM] + [VMEM] * 3 + [ANY],
    )(lengths, cot_own, cot_got, next_half, token)
    far_back, far_cross = along_z(back, 1), along_z_crossed(back)
    wide = call(
        split_wide, shape(2 * UP, HALF), in_specs=[SMEM, VMEM, VMEM, ANY], cost=0.01,
    )(core, gate_weight.T, up_weight.T, back)
    near = call(
        near_terms, shape(2 * CAP + HEAD, 2 * UP + 128, kind=F32),
        cost=0.01, in_specs=[VMEM] * 8,
    )(head, tail, far_head, cot_own, cot_got, cot_tail, wide, half)
    near_other = between_cores(near)
    gate_near, up_near, early = call(
        near_grads,
        (shape(2 * CAP, HB), shape(2 * CAP, HB), shape(2 * CAP, 2 * UP, kind=F32)),
        cost=0.3, in_specs=[SMEM] + [VMEM] * 2,
    )(core, near, near_other)
    far = call(
        far_terms, shape(CAP + TAIL, 2 * UP), cost=10, in_specs=[VMEM] * 2
    )(far_tail, wide)
    far_other = between_cores(far)

    grads = call(
        weight_grads, shape(FIRST, 2 * HB, HALF // FIRST), cost=2.1, in_specs=[SMEM] + [VMEM] * 11,
    )(core, early, far, far_other, far_back, far_cross, gate_near, up_near, head, tail, far_head, far_tail)
    grads = lax.all_to_all(grads, ("xh", "xl", "yl"), split_axis=0, concat_axis=0, tiled=True)
    grads = call(
        first_sum, shape(SECOND, HB, 128), cost=0.4,
    )(grads)
    grads = lax.all_to_all(grads, "yh", split_axis=0, concat_axis=0, tiled=True)
    return call(
        second_sum, (shape(64, HB, kind=F32), shape(64, HB, kind=F32)),
                in_specs=[VMEM],
    )(grads)


def solution(mesh):
    planes = mesh.shape["blk"]
    names = ("z", "xl", "yh", "yl", "xh", "c")
    fine = Mesh(mesh.devices.reshape(planes, 2, 4, 2, 2, 2), names)
    rows = P(names, None)
    placed = (rows, rows, P(None, "z"), P(None, "z"), P("z", None), rows, rows)
    out = P(names[1:], "z")
    return jax.shard_map(
        on_device, mesh=fine, in_specs=placed, out_specs=(out, out), check_vma=False
    )
```
